32 devices in a mesh: dp: 4 (over z), ctx: 4 (over y, x), tp: 2 (over core).
Axes of the slice: x: 2, y: 2, z: 4, core: 2. Of those that a mesh axis runs over, the one named last changes fastest.
Arguments:
- tokens: bfloat16 [8, 1024, 1024], P('dp', 'ctx'), may hold values from -6 to 6
- segment_ids: int32 [8, 1024], P('dp', 'ctx'), may hold values from 0 to 3, as said below
- out_grad: bfloat16 [8, 1024, 1024], P('dp', 'ctx'), may hold values from -6 to 6
- attn_gain: bfloat16 [1024], P(('dp', 'ctx')), may hold values from 0.5 to 1.5
- ffn_gain: bfloat16 [1024], P(('dp', 'ctx')), may hold values from 0.5 to 1.5
- attention_input_weight: bfloat16 [1024, 768], P(('dp', 'ctx'), 'tp'), may hold values from -0.1875 to 0.1875
- state_space_input_weight: bfloat16 [1024, 3072], P(('dp', 'ctx'), 'tp'), may hold values from -0.1875 to 0.1875
- scan_input_weight: bfloat16 [1024, 280], P(('dp', 'ctx')), may hold values from -0.1875 to 0.1875
- mixer_output_weight: bfloat16 [1024, 2048], P(('dp', 'ctx'), 'tp'), may hold values from -0.125 to 0.125
- gate_up_weight: bfloat16 [1024, 4096], P(('dp', 'ctx'), 'tp'), may hold values from -0.1875 to 0.1875
- down_weight_matrix: bfloat16 [1024, 2048], P(('dp', 'ctx'), 'tp'), may hold values from -0.125 to 0.125
- log_decay: float32 [24], P('tp'), may hold values from -4.6 to 0
- step_bias: float32 [24], P('tp'), may hold values from -6.9 to -2.3
- skip_gain: float32 [24], P('tp'), may hold values from 0.5 to 1.5
- conv_x_weight: float32 [4, 1536], P(None, 'tp'), may hold values from -3 to 3
- conv_x_bias: float32 [1536], P('tp'), may hold values from -0.5 to 0.5
- conv_bc_weight: float32 [4, 256], replicated, may hold values from -3 to 3
- conv_bc_bias: float32 [256], replicated, may hold values from -0.5 to 0.5
Outputs:
- layer_out: bfloat16 [8, 1024, 1024], P('dp', 'ctx')
- tokens_grad: float32 [8, 1024, 1024], P('dp', 'ctx')
- attn_gain_grad: float32 [1024], P(('dp', 'ctx'))
- ffn_gain_grad: float32 [1024], P(('dp', 'ctx'))
- attn_in_grad: float32 [1024, 768], P(('dp', 'ctx'), 'tp')
- ssm_in_grad: float32 [1024, 3072], P(('dp', 'ctx'), 'tp')
- scan_in_grad: float32 [1024, 280], P(('dp', 'ctx'))
- mixer_out_grad: float32 [1024, 2048], P(('dp', 'ctx'), 'tp')
- gate_up_grad: float32 [1024, 4096], P(('dp', 'ctx'), 'tp')
- down_proj_grad: float32 [1024, 2048], P(('dp', 'ctx'), 'tp')
- log_decay_grad: float32 [24], P('tp')
- step_bias_grad: float32 [24], P('tp')
- skip_gain_grad: float32 [24], P('tp')
- conv_x_weight_grad: float32 [4, 1536], P(None, 'tp')
- conv_x_bias_grad: float32 [1536], P('tp')
- conv_bc_weight_grad: float32 [4, 256], replicated
- conv_bc_bias_grad: float32 [256], replicated
The draws below stay inside these ranges and needn't reach their ends.
Inputs may be any that keep to these rules, and one draw needn't show every extreme that they name: `segment_ids`: in each sequence the ids start at 0, never fall, and rise by one at a boundary; one document starts within the first 256 positions and ends within the last 256.
All inputs are finite; a program needn't handle non-finite values.
Results may differ from the reference program's by a relative error of at most 0.018.
Values may be sent and summed in bfloat16 or wider, within the bound.
A program may use at most 128 MiB of HBM per device.

```python
import math
import jax
import jax.numpy as jnp
from jax import lax

D = 1024
HEADS = 8
KV_HEADS = 2
HEAD_SIZE = 64
M_HEADS = 24
M_HEAD = 64
STATE = 128
FF = 2048
CONV = 4
TOK_SEQ = 256
SEQS = 8
LEN = 1024
N_TP = 2


def draw_segment_ids(key, part):
    key = jax.random.fold_in(key, 7)
    split_keys = jax.random.split(key, 3)
    early = jax.random.randint(split_keys[0], (SEQS, 1), 1, TOK_SEQ // 2)
    middle_state = jax.random.randint(split_keys[1], (SEQS, 1), TOK_SEQ // 2, TOK_SEQ)
    closing = jax.random.randint(split_keys[2], (SEQS, 1), LEN - TOK_SEQ + 1, LEN)
    positions = jnp.arange(LEN, dtype=jnp.int32)[None, :]
    return (positions >= early).astype(jnp.int32) + (positions >= middle_state).astype(jnp.int32) + (positions >= closing).astype(jnp.int32)


def levels(rng, extent, cuts, smallest, largest):
    factor_of = 1.0
    for dim, parts in cuts:
        heights = jax.random.uniform(jax.random.fold_in(jax.random.fold_in(rng, 6), dim), (parts,), jnp.float32, smallest / len(cuts), largest / len(cuts))
        factor_of = factor_of * jnp.repeat(jnp.exp(heights), extent[dim] // parts).reshape((-1,) + (1,) * (len(extent) - 1 - dim))
    return factor_of


def bell_draw(rng, dims, scale, most, shards=(), kind=jnp.bfloat16):
    loudness = levels(rng, dims, shards, -0.22, 0.18) if shards else 1.0
    values = jax.random.normal(rng, dims, jnp.float32) * scale * loudness
    return jnp.minimum(jnp.maximum(values, -most), most).astype(kind)


def setup_inputs(seed: int = 0) -> dict:
    splits = jax.random.split(jax.random.key(seed), 19)
    tokens = bell_draw(splits[0], (SEQS, LEN, D), 1.0, 6.0, ((0, 4), (1, 4)))
    segment_ids = draw_segment_ids(jax.random.fold_in(splits[18], 71), 0)
    out_grad = bell_draw(splits[2], (SEQS, LEN, D), 1.0, 6.0, ((0, 4), (1, 4)))
    attn_gain = jnp.clip(1.0 + 0.1 * jax.random.normal(splits[3], (D,), jnp.float32), 0.5, 1.5).astype(jnp.bfloat16)
    ffn_gain = jnp.clip(1.0 + 0.1 * jax.random.normal(splits[4], (D,), jnp.float32), 0.5, 1.5).astype(jnp.bfloat16)
    attention_input_weight = bell_draw(splits[5], (D, (HEADS + 2 * KV_HEADS) * HEAD_SIZE), D ** -0.5, 0.1875, ((0, 16), (1, 2)))
    state_space_input_weight = bell_draw(splits[6], (D, 2 * M_HEADS * M_HEAD), D ** -0.5, 0.1875, ((0, 16), (1, 2)))
    scan_input_weight = bell_draw(splits[7], (D, 2 * STATE + M_HEADS), D ** -0.5, 0.1875, ((0, 16),))
    mixer_output_weight = bell_draw(splits[8], (D, M_HEADS * M_HEAD + HEADS * HEAD_SIZE), (M_HEADS * M_HEAD + HEADS * HEAD_SIZE) ** -0.5, 0.125, ((0, 16), (1, 2)))
    gate_up_weight = bell_draw(splits[9], (D, 2 * FF), D ** -0.5, 0.1875, ((0, 16), (1, 2)))
    down_weight_matrix = bell_draw(splits[10], (D, FF), FF ** -0.5, 0.125, ((0, 16), (1, 2)))
    log_decay = jnp.clip(-4.6 + 4.6 * jax.random.uniform(splits[11], (M_HEADS,), jnp.float32) ** levels(splits[11], (M_HEADS,), ((0, 2),), -0.2, 0.2), -4.6, 0.0)
    step_bias = jnp.clip(-6.9 + 4.6000001430511475 * jax.random.uniform(splits[12], (M_HEADS,), jnp.float32) ** levels(splits[12], (M_HEADS,), ((0, 2),), -0.2, 0.2), -6.9, -2.3)
    skip_gain = jnp.clip(0.5 + 1.0 * jax.random.uniform(splits[13], (M_HEADS,), jnp.float32) ** levels(splits[13], (M_HEADS,), ((0, 2),), -0.2, 0.2), 0.5, 1.5)
    conv_x_weight = bell_draw(splits[14], (CONV, M_HEADS * M_HEAD), CONV ** -0.5, 3.0, ((1, 2),), jnp.float32)
    conv_x_bias = jnp.clip(jax.random.uniform(splits[15], (M_HEADS * M_HEAD,), jnp.float32, -0.5, 0.5) * levels(splits[15], (M_HEADS * M_HEAD,), ((0, 2),), -0.4, 0.0), -0.5, 0.5)
    conv_bc_weight = bell_draw(splits[16], (CONV, 2 * STATE), CONV ** -0.5, 3.0, (), jnp.float32)
    conv_bc_bias = jnp.clip(jax.random.uniform(splits[17], (2 * STATE,), jnp.float32, -0.5, 0.5), -0.5, 0.5)
    return dict(tokens=tokens, segment_ids=segment_ids, out_grad=out_grad, attn_gain=attn_gain, ffn_gain=ffn_gain, attention_input_weight=attention_input_weight, state_space_input_weight=state_space_input_weight, scan_input_weight=scan_input_weight, mixer_output_weight=mixer_output_weight, gate_up_weight=gate_up_weight, down_weight_matrix=down_weight_matrix, log_decay=log_decay, step_bias=step_bias, skip_gain=skip_gain, conv_x_weight=conv_x_weight, conv_x_bias=conv_x_bias, conv_bc_weight=conv_bc_weight, conv_bc_bias=conv_bc_bias)


epsilon = 1e-05
rope_base = 100000000000.0
big_negative = -1e+30
highest = lax.Precision.HIGHEST

@jax.custom_vjp
def low(v):
    return lax.optimization_barrier(v.astype(jnp.bfloat16)).astype(jnp.float32)

@jax.custom_vjp
def slice_backward(v):
    return v

def low_keep(v):
    return (low(v), None)

def low_pass(kept, grad):
    return (grad,)

def back_keep(v):
    return (v, None)

def back_low(kept, grad):
    return (low(grad),)
low.defvjp(low_keep, low_pass)
slice_backward.defvjp(back_keep, back_low)

def matrix_product(form, left, right):
    return jnp.einsum(form, left, right, precision=highest)

def rms_norm(values, gain_vec):
    return values * lax.rsqrt(lax.optimization_barrier(jnp.mean(values * values, -1, keepdims=True)) + epsilon) * gain_vec

def rotate(values, cosine, sine_part):
    half_dim = values.shape[-1] // 2
    front, back_half = (values[..., :half_dim], values[..., half_dim:])
    return jnp.concatenate([front * cosine - back_half * sine_part, back_half * cosine + front * sine_part], -1)

def causal_conv(values, weight, bias, seg_ids):
    sequence_length = values.shape[1]
    reach = CONV - 1
    padded = jnp.pad(values, ((0, 0), (reach, 0), (0, 0)))
    padded_seg = jnp.pad(seg_ids, ((0, 0), (reach, 0)), constant_values=-1)
    total = bias
    for lag in range(CONV):
        start = reach - lag
        same = (padded_seg[:, start:start + sequence_length] == seg_ids).astype(jnp.float32)
        total = total + weight[lag] * padded[:, start:start + sequence_length] * same[..., None]
    return total

def attention(query_slice, key_low, value_low, seg_ids):
    query_groups, sequence_length = seg_ids.shape
    block_len = min(512, sequence_length)
    block_count = sequence_length // block_len
    key_pos = jnp.arange(sequence_length, dtype=jnp.int32)

    def one_block(block_index):
        row_start = block_index * block_len
        row_block = lax.dynamic_slice_in_dim(query_slice, row_start, block_len, 1)
        row_seg = lax.dynamic_slice_in_dim(seg_ids, row_start, block_len, 1)
        row_pos = row_start + jnp.arange(block_len, dtype=jnp.int32)
        allowed = (key_pos[None, None, :] <= row_pos[None, :, None]) & (row_seg[:, :, None] == seg_ids[:, None, :])
        raw_scores = slice_backward(matrix_product('gqkhe,gske->gkhqs', row_block, key_low)) * HEAD_SIZE ** (-0.5)
        raw_scores = jnp.where(allowed[:, None, None], raw_scores, big_negative)
        probability_slice = low(jax.nn.softmax(raw_scores, -1))
        return slice_backward(matrix_product('gkhqs,gske->gqkhe', probability_slice, value_low))
    outputs = lax.map(jax.checkpoint(one_block), jnp.arange(block_count, dtype=jnp.int32))
    return jnp.moveaxis(outputs, 0, 1).reshape(query_slice.shape)

def block_step(carry, pieces):
    state_before, seg_before = carry
    xs_block, b_block, c_block, step_block, log_block, seg_block = pieces
    cumulative = jnp.cumsum(log_block, 1)
    cum_heads = jnp.moveaxis(cumulative, 2, 1)
    step_heads = jnp.moveaxis(step_block, 2, 1)
    block_len = seg_block.shape[1]
    causal = jnp.arange(block_len, dtype=jnp.int32)[:, None] >= jnp.arange(block_len, dtype=jnp.int32)[None, :]
    same_doc = (seg_block[:, :, None] == seg_block[:, None, :]) & causal[None]
    allowed = same_doc[:, None]
    gap = cum_heads[:, :, :, None] - cum_heads[:, :, None, :]
    expo = jnp.where(allowed, jnp.exp(jnp.where(allowed, gap, 0.0)), 0.0)
    pair = slice_backward(matrix_product('gtn,gsn->gts', c_block, b_block))
    mix_matrix = low(expo * pair[:, None] * step_heads[:, :, None, :])
    intra_term = matrix_product('ghts,gshp->gthp', mix_matrix, xs_block)
    entry_decay = jnp.exp(cumulative) * (seg_block == seg_before[:, None]).astype(jnp.float32)[:, :, None]
    inter_term = slice_backward(matrix_product('gtn,ghpn->gthp', c_block, low(state_before)))
    ssm_vals = slice_backward(intra_term + entry_decay[..., None] * inter_term)
    end_weight = jnp.exp(cumulative[:, -1:] - cumulative) * (seg_block == seg_block[:, -1:]).astype(jnp.float32)[:, :, None] * step_block
    weighted = low(xs_block * end_weight[..., None])
    local_state = slice_backward(matrix_product('gshp,gsn->ghpn', weighted, b_block))
    passing = (seg_block[:, -1] == seg_before).astype(jnp.float32)[:, None] * jnp.exp(cumulative[:, -1])
    state_after = local_state + passing[:, :, None, None] * state_before
    return ((state_after, seg_block[:, -1]), ssm_vals)

def mamba(xs_vals, z_vals, bc_vals, step_raw, seg_ids, log_decay, step_bias, skip_gain, conv_x_weight, conv_x_bias, conv_bc_weight, conv_bc_bias):
    query_groups, sequence_length = seg_ids.shape
    conv_x = causal_conv(low(xs_vals.reshape(query_groups, sequence_length, -1)), conv_x_weight, conv_x_bias, seg_ids)
    xs_low = low(jax.nn.silu(conv_x)).reshape(xs_vals.shape)
    conv_bc = causal_conv(low(bc_vals), conv_bc_weight, conv_bc_bias, seg_ids)
    bc_low = low(jax.nn.silu(conv_bc))
    b_low = bc_low[..., :STATE]
    c_low = bc_low[..., STATE:]
    seg_float = seg_ids.astype(jnp.float32)
    step_size = jax.nn.softplus(step_raw + step_bias)
    log_step = -jnp.exp(log_decay) * step_size
    block_count = sequence_length // TOK_SEQ

    def split(values):
        return jnp.moveaxis(values.reshape((query_groups, block_count, TOK_SEQ) + values.shape[2:]), 1, 0)
    start = (jnp.zeros((query_groups, M_HEADS, M_HEAD, STATE), jnp.float32), -jnp.ones((query_groups,), jnp.float32))
    pieces = (split(xs_low), split(b_low), split(c_low), split(step_size), split(log_step), split(seg_float))
    _, ssm_blocks = lax.scan(jax.checkpoint(block_step), start, pieces)
    ssm_vals = jnp.moveaxis(ssm_blocks, 0, 1).reshape(xs_vals.shape)
    return (ssm_vals + skip_gain[:, None] * xs_low) * jax.nn.silu(z_vals)

def layer(layer_inputs, seg_ids, attn_gain, ffn_gain, attention_input_weight, state_space_input_weight, scan_input_weight, mixer_output_weight, gate_up_weight, down_weight_matrix, log_decay, step_bias, skip_gain, conv_x_weight, conv_x_bias, conv_bc_weight, conv_bc_bias):
    query_groups, sequence_length, model_width = layer_inputs.shape
    head_group = HEADS // KV_HEADS
    query_width = head_group * HEAD_SIZE
    first_norm_slice = low(rms_norm(layer_inputs, attn_gain))
    query_key_value = slice_backward(matrix_product('kfn,ni->kfi', first_norm_slice, attention_input_weight)).reshape(query_groups, sequence_length, N_TP, -1)
    query_vals = query_key_value[..., :query_width].reshape(query_groups, sequence_length, N_TP, head_group, HEAD_SIZE)
    key_vals = query_key_value[..., query_width:query_width + HEAD_SIZE]
    value_vals = query_key_value[..., query_width + HEAD_SIZE:]
    half_dim = HEAD_SIZE // 2
    frequency = rope_base ** (-jnp.arange(half_dim, dtype=jnp.float32) * 2.0 / HEAD_SIZE)
    angles = jnp.arange(sequence_length, dtype=jnp.float32)[:, None] * frequency[None, :]
    cosine, sine_part = (jnp.cos(angles), jnp.sin(angles))
    query_slice = low(rotate(query_vals, cosine[None, :, None, None], sine_part[None, :, None, None]))
    key_low = low(rotate(key_vals, cosine[None, :, None], sine_part[None, :, None]))
    value_low = low(value_vals)
    attn_vals = attention(query_slice, key_low, value_low, seg_ids)
    gate_input_values = slice_backward(matrix_product('kfn,ni->kfi', first_norm_slice, state_space_input_weight)).reshape(query_groups, sequence_length, N_TP, 2, -1)
    z_vals = gate_input_values[:, :, :, 0].reshape(query_groups, sequence_length, M_HEADS, M_HEAD)
    xs_vals = gate_input_values[:, :, :, 1].reshape(query_groups, sequence_length, M_HEADS, M_HEAD)
    scan_input_values = slice_backward(matrix_product('kfn,ni->kfi', first_norm_slice, scan_input_weight))
    mamba_out = mamba(xs_vals, z_vals, scan_input_values[..., :2 * STATE], scan_input_values[..., 2 * STATE:], seg_ids, log_decay, step_bias, skip_gain, conv_x_weight, conv_x_bias, conv_bc_weight, conv_bc_bias)
    joined = jnp.concatenate([mamba_out.reshape(query_groups, sequence_length, N_TP, -1), attn_vals.reshape(query_groups, sequence_length, N_TP, -1)], -1)
    mixer_slice = low(joined.reshape(query_groups, sequence_length, -1))
    middle_state = layer_inputs + slice_backward(matrix_product('efv,hv->efh', mixer_slice, mixer_output_weight))
    second_norm_slice = low(rms_norm(middle_state, ffn_gain))
    gate_values = slice_backward(matrix_product('kfn,ni->kfi', second_norm_slice, gate_up_weight)).reshape(query_groups, sequence_length, N_TP, 2, -1)
    activation_slice = low((jax.nn.silu(gate_values[:, :, :, 0]) * gate_values[:, :, :, 1]).reshape(query_groups, sequence_length, -1))
    return middle_state + slice_backward(matrix_product('efv,hv->efh', activation_slice, down_weight_matrix))

def reference(tokens, segment_ids, out_grad, attn_gain, ffn_gain, attention_input_weight, state_space_input_weight, scan_input_weight, mixer_output_weight, gate_up_weight, down_weight_matrix, log_decay, step_bias, skip_gain, conv_x_weight, conv_x_bias, conv_bc_weight, conv_bc_bias):
    params = tuple((item.astype(jnp.float32) for item in (attn_gain, ffn_gain, attention_input_weight, state_space_input_weight, scan_input_weight, mixer_output_weight, gate_up_weight, down_weight_matrix, log_decay, step_bias, skip_gain, conv_x_weight, conv_x_bias, conv_bc_weight, conv_bc_bias)))
    sequences, sequence_length = segment_ids.shape
    per_step = math.gcd(sequences, max(1, 4096 // sequence_length))
    step_count = sequences // per_step

    def grouped(values):
        return values.reshape((step_count, per_step) + values.shape[1:])

    def one_step(totals, pieces):
        layer_inputs, seg_ids, cotangent = pieces

        def apply(values, *weights):
            return layer(values, seg_ids, *weights)
        outputs, pullback = jax.vjp(apply, layer_inputs.astype(jnp.float32), *params)
        grads = pullback(cotangent.astype(jnp.float32))
        return (jax.tree.map(jnp.add, totals, tuple(grads[1:])), (outputs.astype(jnp.bfloat16), grads[0]))
    zeros = tuple((jnp.zeros_like(item) for item in params))
    totals, (outputs, input_grads) = lax.scan(one_step, zeros, (grouped(tokens), grouped(segment_ids), grouped(out_grad)))
    g_attn_gain, g_ffn_gain, g_attn_in, g_ssm_in, g_scan_in, g_mixer_out, g_gate_up, g_down_proj, g_log_decay, g_step_bias, g_skip_gain, g_conv_x_weight, g_conv_x_bias, g_conv_bc_weight, g_conv_bc_bias = totals
    return (outputs.reshape(tokens.shape), input_grads.reshape(tokens.shape), g_attn_gain, g_ffn_gain, g_attn_in, g_ssm_in, g_scan_in, g_mixer_out, g_gate_up, g_down_proj, g_log_decay, g_step_bias, g_skip_gain, g_conv_x_weight, g_conv_x_bias, g_conv_bc_weight, g_conv_bc_bias)
```

```python
import jax
import jax.numpy as jnp
from jax import lax
from jax.sharding import PartitionSpec as P

HEADS = 8
HEAD_SIZE = 64
M_HEADS = 24
M_HEAD = 64
STATE = 128
FF = 2048


epsilon = 1e-05
rope_base = 100000000000.0
big_negative = -1e30


def carried_in(array, axis, combine, identity):
    count, mine = (lax.axis_size(axis), lax.axis_index(axis))
    everything = jax.tree.map(
        lambda part, kind: lax.all_gather(part.astype(kind), axis),
        array,
        (jnp.bfloat16, jnp.bfloat16, jnp.bfloat16, jnp.bfloat16),
    )
    start = jax.tree.map(
        lambda part, zero: jnp.broadcast_to(jnp.asarray(zero, part.dtype), part.shape),
        array,
        identity,
    )

    def step(k, before):
        reached = k < mine
        new = combine(
            before, jax.tree.map(lambda part, own: part[k].astype(own.dtype), everything, array)
        )
        return jax.tree.map(lambda a, b: jnp.where(reached, a, b), new, before)

    return lax.fori_loop(0, count, step, start)


def prefix(array, axis, join, neutral):
    count = lax.axis_size(axis)
    place = lax.axis_index(axis)
    ahead = count - 1 - place
    gathered = jax.tree.map(
        lambda a, kind: lax.all_gather(a.astype(kind), axis), array, (jnp.bfloat16, jnp.bfloat16)
    )
    state = jax.tree.map(lambda a, e: jnp.zeros_like(a) + jnp.asarray(e, a.dtype), array, neutral)

    def one(step, state):
        source = count - 1 - step
        return join(
            state,
            jax.tree.map(
                lambda a, own: lax.dynamic_index_in_dim(a, source, 0, False).astype(own.dtype),
                gathered,
                array,
            ),
        )

    return lax.fori_loop(0, ahead, one, state)


def shifted(value, axis, steps):
    count = lax.axis_size(axis)
    initial, last = (max(0, -steps), min(count, count - steps))
    return lax.ppermute(value, axis, [(source, source + steps) for source in range(initial, last)])


def pair_sum(partial):
    low = partial.astype(jnp.bfloat16)
    if lax.axis_size("tp") != 2:
        return lax.psum(low, "tp").astype(jnp.float32)
    other = lax.ppermute(low, "tp", [(0, 1), (1, 0)])
    return low.astype(jnp.float32) + other.astype(jnp.float32)


def gather_rows(*shards):
    return [lax.all_gather(shard, ("dp", "ctx"), axis=0, tiled=True) for shard in shards]


def scatter_rows(*partials):
    return [
        lax.psum_scatter(part, ("dp", "ctx"), scatter_dimension=0, tiled=True).astype(jnp.float32)
        for part in partials
    ]


def rms_scale(values):
    return lax.rsqrt(jnp.mean(values * values, -1, keepdims=True) + epsilon)


def norm_back(grad_out, normed, row_scale, gain_vec):
    grad_normed = grad_out * gain_vec
    return row_scale * (grad_normed - normed * jnp.mean(grad_normed * normed, -1, keepdims=True))


def rotate(values, cosine, sine_part):
    half_dim = values.shape[-1] // 2
    front, back_half = (values[..., :half_dim], values[..., half_dim:])
    return jnp.concatenate(
        [front * cosine - back_half * sine_part, back_half * cosine + front * sine_part], -1
    )


def silu_slope(values):
    sigmoid_vals = jax.nn.sigmoid(values)
    return sigmoid_vals * (1.0 + values * (1.0 - sigmoid_vals))


def conv_forward(extended, own_seg, seg_before_ext, weight, bias, count):
    reach = weight.shape[0] - 1
    total = bias
    for lag in range(reach + 1):
        start = reach - lag
        same = (seg_before_ext[:, start : start + count] == own_seg).astype(jnp.float32)
        total = total + weight[lag] * extended[:, start : start + count] * same[..., None]
    return total


def conv_backward(grad_ext, extended, own_seg, seg_before_ext, seg_after_ext, weight, count):
    reach = weight.shape[0] - 1
    own_grad = grad_ext[:, :count]
    input_grad = jnp.zeros_like(own_grad)
    tap_grads = []
    for lag in range(reach + 1):
        ahead = (seg_after_ext[:, lag : lag + count] == own_seg).astype(jnp.float32)
        input_grad = input_grad + weight[lag] * grad_ext[:, lag : lag + count] * ahead[..., None]
        start = reach - lag
        behind = (seg_before_ext[:, start : start + count] == own_seg).astype(jnp.float32)
        tap_grads.append(
            jnp.sum(own_grad * extended[:, start : start + count] * behind[..., None], (0, 1))
        )
    return (input_grad, jnp.stack(tap_grads), jnp.sum(own_grad, (0, 1)))


def link_states(early_part, late_part):
    early_first, early_last, early_gate, early_state = early_part
    late_first, late_last, late_gate, late_state = late_part
    joined = ((early_last == late_first) | (early_last < -0.5) | (late_first < -0.5)).astype(
        jnp.float32
    )
    first_seg = jnp.where(early_first < -0.5, late_first, early_first)
    last_seg = jnp.where(late_last < -0.5, early_last, late_last)
    passing = late_gate * joined[:, None]
    return (
        first_seg,
        last_seg,
        early_gate * passing,
        late_state + passing[:, :, None, None] * early_state,
    )


def link_grads(early_part, late_part):
    early_gate, early_grad = early_part
    late_gate, late_grad = late_part
    return (early_gate * late_gate, late_grad + late_gate[:, :, None, None] * early_grad)


def per_device(
    tokens,
    segment_ids,
    out_grad,
    attn_gain,
    ffn_gain,
    attention_input_weight,
    state_space_input_weight,
    scan_input_weight,
    mixer_output_weight,
    gate_up_weight,
    down_weight_matrix,
    log_decay,
    step_bias,
    skip_gain,
    conv_x_weight,
    conv_x_bias,
    conv_bc_weight,
    conv_bc_bias,
):
    single_layer = jnp.float32
    narrow_slice = jnp.bfloat16
    tp_count = lax.axis_size("tp")
    ctx_count = lax.axis_size("ctx")
    tp_index = lax.axis_index("tp")
    ctx_index = lax.axis_index("ctx")
    sequences, tok_count, model_width = tokens.shape
    head_count = HEADS // tp_count
    mamba_count = M_HEADS // tp_count
    query_width = head_count * HEAD_SIZE
    mamba_width = mamba_count * M_HEAD
    ffn_width = FF // tp_count
    row_count = tok_count * head_count
    score_scale = HEAD_SIZE ** (-0.5)
    reach = conv_x_weight.shape[0] - 1
    qkv_width = attention_input_weight.shape[1]
    zx_width = state_space_input_weight.shape[1]
    bcd_width = scan_input_weight.shape[1]
    first_pad = -(qkv_width + zx_width + bcd_width + 2) % 128
    first_shard = jnp.concatenate(
        [
            state_space_input_weight,
            attention_input_weight,
            scan_input_weight,
            attn_gain[:, None],
            ffn_gain[:, None],
            jnp.zeros((attn_gain.shape[0], first_pad), narrow_slice),
        ],
        1,
    )
    full_first, full_mix, full_gu, full_down = gather_rows(
        first_shard, mixer_output_weight, gate_up_weight, down_weight_matrix
    )
    first_width = qkv_width + zx_width + bcd_width
    full_zx = full_first[:, :zx_width]
    full_qkv = full_first[:, zx_width : zx_width + qkv_width]
    full_bcd = full_first[:, zx_width + qkv_width : first_width]
    gain_one = full_first[:, first_width].astype(single_layer)
    gain_two = full_first[:, first_width + 1].astype(single_layer)
    layer_inputs = tokens.astype(single_layer)
    first_scale = rms_scale(layer_inputs)
    first_normed = layer_inputs * first_scale
    first_norm_slice = (first_normed * gain_one).astype(narrow_slice)
    qkv_vals = jnp.einsum(
        "btd,dc->btc", first_norm_slice, full_qkv, preferred_element_type=single_layer
    )
    gate_input_values = jnp.einsum(
        "btd,dc->btc", first_norm_slice, full_zx, preferred_element_type=single_layer
    )
    scan_input_values = jnp.einsum(
        "btd,dc->btc", first_norm_slice, full_bcd, preferred_element_type=single_layer
    )
    half_dim = HEAD_SIZE // 2
    frequency = rope_base ** (-jnp.arange(half_dim, dtype=single_layer) * 2.0 / HEAD_SIZE)
    positions = (ctx_index * tok_count + jnp.arange(tok_count, dtype=jnp.int32)).astype(
        single_layer
    )
    angles = positions[:, None] * frequency[None, :]
    cosine, sine_part = (jnp.cos(angles), jnp.sin(angles))
    query_rot = rotate(
        qkv_vals[..., :query_width].reshape(sequences, tok_count, head_count, HEAD_SIZE),
        cosine[None, :, None],
        sine_part[None, :, None],
    )
    query_slice = query_rot.astype(narrow_slice).reshape(sequences, row_count, HEAD_SIZE)
    key_rot = rotate(
        qkv_vals[..., query_width : query_width + HEAD_SIZE], cosine[None], sine_part[None]
    )
    key_value = jnp.concatenate([key_rot, qkv_vals[..., query_width + HEAD_SIZE :]], -1).astype(
        narrow_slice
    )
    seg_float = segment_ids.astype(single_layer)
    conv_x_in = gate_input_values[..., mamba_width:].astype(narrow_slice)
    conv_bc_in = scan_input_values[..., : 2 * STATE].astype(narrow_slice)
    all_kv, all_seg, tails_x, tails_bc = (
        lax.all_gather(key_value, "ctx", axis=1, tiled=True),
        lax.all_gather(seg_float.astype(narrow_slice), "ctx", axis=1, tiled=True),
        lax.all_gather(conv_x_in[:, tok_count - reach :], "ctx", axis=1, tiled=True),
        lax.all_gather(conv_bc_in[:, tok_count - reach :], "ctx", axis=1, tiled=True),
    )
    full_len = all_kv.shape[1]
    seg_all = all_seg.astype(single_layer)
    has_prev = ctx_index > 0
    has_next = ctx_index < ctx_count - 1
    prev_index = jnp.maximum(ctx_index - 1, 0)
    prev_x = lax.dynamic_slice_in_dim(tails_x, prev_index * reach, reach, 1)
    prev_bc = lax.dynamic_slice_in_dim(tails_bc, prev_index * reach, reach, 1)
    prev_x = jnp.where(has_prev, prev_x, jnp.zeros_like(prev_x))
    prev_bc = jnp.where(has_prev, prev_bc, jnp.zeros_like(prev_bc))
    prev_seg = lax.dynamic_slice_in_dim(
        seg_all, jnp.maximum(ctx_index * tok_count - reach, 0), reach, 1
    )
    prev_seg = jnp.where(has_prev, prev_seg, -jnp.ones_like(prev_seg))
    next_seg = lax.dynamic_slice_in_dim(
        seg_all, jnp.minimum((ctx_index + 1) * tok_count, full_len - reach), reach, 1
    )
    next_seg = jnp.where(has_next, next_seg, -jnp.ones_like(next_seg))
    seg_before_ext = jnp.concatenate([prev_seg, seg_float], 1)
    seg_after_ext = jnp.concatenate([seg_float, next_seg], 1)
    ext_x = jnp.concatenate([prev_x, conv_x_in], 1).astype(single_layer)
    ext_bc = jnp.concatenate([prev_bc, conv_bc_in], 1).astype(single_layer)
    conv_x_pre = conv_forward(
        ext_x, seg_float, seg_before_ext, conv_x_weight, conv_x_bias, tok_count
    )
    conv_bc_pre = conv_forward(
        ext_bc, seg_float, seg_before_ext, conv_bc_weight, conv_bc_bias, tok_count
    )
    block_len = min(512, full_len)
    needed = ((ctx_index + 1) * tok_count + block_len - 1) // block_len
    row_pos = ctx_index * tok_count + jnp.arange(row_count, dtype=jnp.int32) // head_count
    row_seg = jnp.repeat(seg_float, head_count, axis=1)

    def block_scores(block_index):
        key_start = block_index * block_len
        key_block_rows = lax.dynamic_slice_in_dim(all_kv, key_start, block_len, 1)
        key_seg = lax.dynamic_slice_in_dim(all_seg, key_start, block_len, 1).astype(single_layer)
        key_pos = key_start + jnp.arange(block_len, dtype=jnp.int32)
        allowed = (key_pos[None, None, :] <= row_pos[None, :, None]) & (
            key_seg[:, None, :] == row_seg[:, :, None]
        )
        raw_scores = (
            jnp.einsum(
                "nwl,nol->nwo",
                query_slice,
                key_block_rows[..., :HEAD_SIZE],
                preferred_element_type=single_layer,
            )
            * score_scale
        )
        return (jnp.where(allowed, raw_scores, big_negative), allowed, key_block_rows)

    def peak_step(block_index, carry):
        row_peak, row_total = carry
        scores, allowed, key_block_rows = block_scores(block_index)
        new_peak = jnp.maximum(row_peak, jnp.max(scores, -1))
        kept = jnp.where(allowed, jnp.exp(scores - new_peak[..., None]), 0.0)
        return (new_peak, row_total * jnp.exp(row_peak - new_peak) + jnp.sum(kept, -1))

    row_peak, row_total = lax.fori_loop(
        0,
        needed,
        peak_step,
        (
            jnp.full((sequences, row_count), big_negative, single_layer),
            jnp.zeros((sequences, row_count), single_layer),
        ),
    )
    log_total = row_peak + jnp.log(row_total)

    def value_step(block_index, accum):
        scores, allowed, key_block_rows = block_scores(block_index)
        probability_slice = jnp.where(allowed, jnp.exp(scores - log_total[..., None]), 0.0).astype(
            narrow_slice
        )
        return accum + jnp.einsum(
            "znw,zwt->znt",
            probability_slice,
            key_block_rows[..., HEAD_SIZE:],
            preferred_element_type=single_layer,
        )

    attn_vals = lax.fori_loop(
        0, needed, value_step, jnp.zeros((sequences, row_count, HEAD_SIZE), single_layer)
    )
    attn_low = attn_vals.astype(narrow_slice).reshape(sequences, tok_count, query_width)
    z_vals = gate_input_values[..., :mamba_width].reshape(sequences, tok_count, mamba_count, M_HEAD)
    xs_low = (
        jax.nn.silu(conv_x_pre)
        .astype(narrow_slice)
        .reshape(sequences, tok_count, mamba_count, M_HEAD)
    )
    xs_vals = xs_low.astype(single_layer)
    bc_low = jax.nn.silu(conv_bc_pre).astype(narrow_slice)
    b_low = bc_low[..., :STATE]
    c_low = bc_low[..., STATE:]
    step_raw = lax.dynamic_slice_in_dim(
        scan_input_values, 2 * STATE + tp_index * mamba_count, mamba_count, 2
    )
    step_size = jax.nn.softplus(step_raw + step_bias)
    decay_rate = jnp.exp(log_decay)
    log_step = -decay_rate * step_size
    cumulative = jnp.cumsum(log_step, 1)
    cum_heads = jnp.moveaxis(cumulative, 2, 1)
    step_heads = jnp.moveaxis(step_size, 2, 1)
    causal = (
        jnp.arange(tok_count, dtype=jnp.int32)[:, None]
        >= jnp.arange(tok_count, dtype=jnp.int32)[None, :]
    )
    same_doc = (seg_float[:, :, None] == seg_float[:, None, :]) & causal[None]
    allowed_heads = same_doc[:, None]
    gap = cum_heads[:, :, :, None] - cum_heads[:, :, None, :]
    expo = jnp.where(allowed_heads, jnp.exp(jnp.where(allowed_heads, gap, 0.0)), 0.0)
    pair = jnp.einsum("btn,bsn->bts", c_low, b_low, preferred_element_type=single_layer)
    mix_matrix = (expo * pair[:, None] * step_heads[:, :, None, :]).astype(narrow_slice)
    intra_term = jnp.einsum(
        "bhts,bshp->bthp", mix_matrix, xs_low, preferred_element_type=single_layer
    )
    end_decay = (
        jnp.exp(cumulative[:, -1:] - cumulative)
        * (seg_float == seg_float[:, -1:]).astype(single_layer)[:, :, None]
    )
    end_weight = end_decay * step_size
    weighted_low = (xs_vals * end_weight[..., None]).astype(narrow_slice)
    local_state = jnp.einsum(
        "bshp,bsn->bhpn", weighted_low, b_low, preferred_element_type=single_layer
    )
    block_gate = (
        jnp.exp(cumulative[:, -1])
        * (seg_float[:, 0] == seg_float[:, -1]).astype(single_layer)[:, None]
    )
    negative = -jnp.ones((sequences,), single_layer)
    identity = (negative, negative, jnp.ones_like(block_gate), jnp.zeros_like(local_state))
    _, seg_before, _, state_before = carried_in(
        (seg_float[:, 0], seg_float[:, -1], block_gate, local_state), "ctx", link_states, identity
    )
    state_low = state_before.astype(narrow_slice)
    inter_term = jnp.einsum("btn,bhpn->bthp", c_low, state_low, preferred_element_type=single_layer)
    entry_decay = (
        jnp.exp(cumulative) * (seg_float == seg_before[:, None]).astype(single_layer)[:, :, None]
    )
    ssm_vals = intra_term + entry_decay[..., None] * inter_term
    mamba_y = ssm_vals + skip_gain[:, None] * xs_vals
    mamba_out = mamba_y * jax.nn.silu(z_vals)
    mixer_slice = jnp.concatenate(
        [mamba_out.reshape(sequences, tok_count, mamba_width).astype(narrow_slice), attn_low], -1
    )
    mix_part = jnp.einsum("btc,dc->btd", mixer_slice, full_mix, preferred_element_type=single_layer)
    middle_state = layer_inputs + pair_sum(mix_part)
    second_scale = rms_scale(middle_state)
    second_normed = middle_state * second_scale
    second_norm_slice = (second_normed * gain_two).astype(narrow_slice)
    gu_vals = jnp.einsum(
        "btd,dc->btc", second_norm_slice, full_gu, preferred_element_type=single_layer
    )
    gate_values, up_vals = (gu_vals[..., :ffn_width], gu_vals[..., ffn_width:])
    activation_slice = (jax.nn.silu(gate_values) * up_vals).astype(narrow_slice)
    ffn_part = jnp.einsum(
        "btc,dc->btd", activation_slice, full_down, preferred_element_type=single_layer
    )
    layer_out = (middle_state + pair_sum(ffn_part)).astype(narrow_slice)
    cotangent = out_grad.astype(single_layer)
    grad_down_w = jnp.einsum(
        "btd,btc->dc", out_grad, activation_slice, preferred_element_type=single_layer
    )
    grad_act = jnp.einsum("btd,dc->btc", out_grad, full_down, preferred_element_type=single_layer)
    grad_gu_low = jnp.concatenate(
        [grad_act * up_vals * silu_slope(gate_values), grad_act * jax.nn.silu(gate_values)], -1
    ).astype(narrow_slice)
    grad_gu_w = jnp.einsum(
        "btd,btc->dc", second_norm_slice, grad_gu_low, preferred_element_type=single_layer
    )
    second_part = jnp.einsum(
        "btc,dc->btd", grad_gu_low, full_gu, preferred_element_type=single_layer
    )
    grad_second = pair_sum(second_part)
    grad_gain_two = jnp.sum(grad_second * second_normed, (0, 1))
    grad_middle = cotangent + norm_back(grad_second, second_normed, second_scale, gain_two)
    grad_mix_low = grad_middle.astype(narrow_slice)
    grad_mix_w = jnp.einsum(
        "btd,btc->dc", grad_mix_low, mixer_slice, preferred_element_type=single_layer
    )
    grad_cat = jnp.einsum(
        "btd,dc->btc", grad_mix_low, full_mix, preferred_element_type=single_layer
    )
    grad_mamba = grad_cat[..., :mamba_width].reshape(sequences, tok_count, mamba_count, M_HEAD)
    attention_gradient_slice = (
        grad_cat[..., mamba_width:].astype(narrow_slice).reshape(sequences, row_count, HEAD_SIZE)
    )
    delta = jnp.sum(attention_gradient_slice.astype(single_layer) * attn_vals, -1)

    def grad_step(block_index, carry):
        grad_query, grad_kv = carry
        scores, allowed, key_block_rows = block_scores(block_index)
        attention_probabilities = jnp.where(allowed, jnp.exp(scores - log_total[..., None]), 0.0)
        grad_probs = jnp.einsum(
            "nwl,nol->nwo",
            attention_gradient_slice,
            key_block_rows[..., HEAD_SIZE:],
            preferred_element_type=single_layer,
        )
        score_gradient = (
            attention_probabilities * (grad_probs - delta[..., None]) * score_scale
        ).astype(narrow_slice)
        grad_query = grad_query + jnp.einsum(
            "znw,zwt->znt",
            score_gradient,
            key_block_rows[..., :HEAD_SIZE],
            preferred_element_type=single_layer,
        )
        grad_keys = jnp.einsum(
            "pni,pnx->pix", score_gradient, query_slice, preferred_element_type=single_layer
        )
        grad_values = jnp.einsum(
            "pni,pnx->pix",
            attention_probabilities.astype(narrow_slice),
            attention_gradient_slice,
            preferred_element_type=single_layer,
        )
        grad_kv = lax.dynamic_update_slice_in_dim(
            grad_kv, jnp.concatenate([grad_keys, grad_values], -1), block_index * block_len, 1
        )
        return (grad_query, grad_kv)

    grad_query, grad_kv = lax.fori_loop(
        0,
        needed,
        grad_step,
        (
            jnp.zeros((sequences, row_count, HEAD_SIZE), single_layer),
            jnp.zeros((sequences, full_len, 2 * HEAD_SIZE), single_layer),
        ),
    )
    own_kv = lax.psum_scatter(
        grad_kv.astype(jnp.bfloat16), "ctx", scatter_dimension=1, tiled=True
    ).astype(jnp.float32)
    query_back = rotate(
        grad_query.reshape(sequences, tok_count, head_count, HEAD_SIZE),
        cosine[None, :, None],
        -sine_part[None, :, None],
    )
    key_back = rotate(own_kv[..., :HEAD_SIZE], cosine[None], -sine_part[None])
    grad_qkv_low = jnp.concatenate(
        [query_back.reshape(sequences, tok_count, query_width), key_back, own_kv[..., HEAD_SIZE:]],
        -1,
    ).astype(narrow_slice)
    sigmoid_z = jax.nn.sigmoid(z_vals)
    grad_y = grad_mamba * z_vals * sigmoid_z
    grad_z = grad_mamba * mamba_y * silu_slope(z_vals)
    grad_skip = jnp.sum(grad_y * xs_vals, (0, 1, 3))
    grad_xs = grad_y * skip_gain[:, None]
    grad_ssm_low = grad_y.astype(narrow_slice)
    grad_matrix = jnp.einsum(
        "bthp,bshp->bhts", grad_ssm_low, xs_low, preferred_element_type=single_layer
    )
    grad_xs = grad_xs + jnp.einsum(
        "bhts,bthp->bshp", mix_matrix, grad_ssm_low, preferred_element_type=single_layer
    )
    shared = grad_matrix * expo
    grad_pair = jnp.sum(shared * step_heads[:, :, None, :], 1)
    grad_step_heads = jnp.sum(shared * pair[:, None], 2)
    grad_gap = shared * pair[:, None] * step_heads[:, :, None, :]
    grad_cum_heads = jnp.sum(grad_gap, 3) - jnp.sum(grad_gap, 2)
    inter_low = (grad_ssm_low.astype(single_layer) * entry_decay[..., None]).astype(narrow_slice)
    grad_entry = jnp.sum(grad_ssm_low.astype(single_layer) * inter_term, -1)
    grad_c = jnp.einsum("bthp,bhpn->btn", inter_low, state_low, preferred_element_type=single_layer)
    grad_state_in = jnp.einsum(
        "bthp,btn->bhpn", inter_low, c_low, preferred_element_type=single_layer
    )
    carry_gate = (seg_float[:, -1] == seg_before).astype(single_layer)[:, None] * jnp.exp(
        cumulative[:, -1]
    )
    _, later_grad = prefix(
        (carry_gate, grad_state_in),
        "ctx",
        link_grads,
        (jnp.ones_like(carry_gate), jnp.zeros_like(grad_state_in)),
    )
    later_low = later_grad.astype(narrow_slice)
    grad_weighted = jnp.einsum(
        "bhpn,bsn->bshp", later_low, b_low, preferred_element_type=single_layer
    )
    grad_b = jnp.einsum(
        "bshp,bhpn->bsn", weighted_low, later_low, preferred_element_type=single_layer
    )
    grad_xs = grad_xs + grad_weighted * end_weight[..., None]
    grad_end = jnp.sum(grad_weighted * xs_vals, -1)
    grad_log_end = grad_end * end_weight
    grad_cum = jnp.moveaxis(grad_cum_heads, 1, 2) + grad_entry * entry_decay - grad_log_end
    grad_cum = grad_cum.at[:, -1].add(
        carry_gate * jnp.sum(later_grad * state_before, (2, 3)) + jnp.sum(grad_log_end, 1)
    )
    pair_low = grad_pair.astype(narrow_slice)
    grad_c = grad_c + jnp.einsum(
        "bts,bsn->btn", pair_low, b_low, preferred_element_type=single_layer
    )
    grad_b = grad_b + jnp.einsum(
        "bts,btn->bsn", pair_low, c_low, preferred_element_type=single_layer
    )
    grad_log_step = jnp.flip(jnp.cumsum(jnp.flip(grad_cum, 1), 1), 1)
    grad_step = (
        jnp.moveaxis(grad_step_heads, 1, 2) + grad_end * end_decay - grad_log_step * decay_rate
    )
    grad_log_decay = jnp.sum(grad_log_step * log_step, (0, 1))
    grad_raw = grad_step * jax.nn.sigmoid(step_raw + step_bias)
    grad_step_bias = jnp.sum(grad_raw, (0, 1))
    grad_steps = lax.dynamic_update_slice_in_dim(
        jnp.zeros((sequences, tok_count, M_HEADS), single_layer),
        grad_raw,
        tp_index * mamba_count,
        2,
    )
    post_x = grad_xs.reshape(sequences, tok_count, mamba_width) * silu_slope(conv_x_pre)
    post_bc = jnp.concatenate([grad_b, grad_c], -1) * silu_slope(conv_bc_pre)
    next_x, next_bc = shifted((post_x[:, :reach], post_bc[:, :reach]), "ctx", -1)
    grad_in_x, conv_x_w_part, conv_x_b_part = conv_backward(
        jnp.concatenate([post_x, next_x], 1),
        ext_x,
        seg_float,
        seg_before_ext,
        seg_after_ext,
        conv_x_weight,
        tok_count,
    )
    grad_zx_low = jnp.concatenate(
        [grad_z.reshape(sequences, tok_count, mamba_width), grad_in_x], -1
    ).astype(narrow_slice)
    first_part = jnp.einsum(
        "btc,dc->btd", grad_qkv_low, full_qkv, preferred_element_type=single_layer
    )
    first_part = first_part + jnp.einsum(
        "btc,dc->btd", grad_zx_low, full_zx, preferred_element_type=single_layer
    )
    first_sum, bc_total, steps_total = (
        pair_sum(first_part),
        pair_sum(jnp.concatenate([post_bc, next_bc], 1)),
        pair_sum(grad_steps),
    )
    grad_in_bc, conv_bc_w_part, conv_bc_b_part = conv_backward(
        bc_total, ext_bc, seg_float, seg_before_ext, seg_after_ext, conv_bc_weight, tok_count
    )
    bcd_low = jnp.concatenate([grad_in_bc, steps_total], -1).astype(narrow_slice)
    grad_first = first_sum + jnp.einsum(
        "btc,dc->btd", bcd_low, full_bcd, preferred_element_type=single_layer
    )
    grad_qkv_w = jnp.einsum(
        "btd,btc->dc", first_norm_slice, grad_qkv_low, preferred_element_type=single_layer
    )
    grad_zx_w = jnp.einsum(
        "btd,btc->dc", first_norm_slice, grad_zx_low, preferred_element_type=single_layer
    )
    grad_bcd_w = jnp.einsum(
        "btd,btc->dc", first_norm_slice, bcd_low, preferred_element_type=single_layer
    )
    grad_gain_one = jnp.sum(grad_first * first_normed, (0, 1))
    tokens_grad = grad_middle + norm_back(grad_first, first_normed, first_scale, gain_one)
    grad_first_w = jnp.concatenate(
        [
            grad_zx_w.astype(narrow_slice),
            grad_qkv_w.astype(narrow_slice),
            grad_bcd_w.astype(narrow_slice),
            grad_gain_one.astype(narrow_slice)[:, None],
            grad_gain_two.astype(narrow_slice)[:, None],
            jnp.zeros((model_width, first_pad), narrow_slice),
        ],
        1,
    )
    first_own, mix_grad, gu_grad, down_grad = scatter_rows(
        grad_first_w,
        grad_mix_w.astype(narrow_slice),
        grad_gu_w.astype(narrow_slice),
        grad_down_w.astype(narrow_slice),
    )
    zx_grad = first_own[:, :zx_width]
    qkv_grad = first_own[:, zx_width : zx_width + qkv_width]
    bcd_grad = first_own[:, zx_width + qkv_width : first_width]
    gain_one_grad = first_own[:, first_width]
    gain_two_grad = first_own[:, first_width + 1]
    small_parts = (
        grad_log_decay,
        grad_step_bias,
        grad_skip,
        conv_x_w_part,
        conv_x_b_part,
        conv_bc_w_part,
        conv_bc_b_part,
    )
    flat = jnp.concatenate([part.reshape(-1) for part in small_parts])
    small_count = flat.shape[0]
    flat = jnp.pad(flat, (0, -small_count % 1024)).reshape(-1, 128)
    small_total = lax.psum(flat, ("dp", "ctx")).reshape(-1)
    small_sums = []
    start = 0
    for part in small_parts:
        small_sums.append(small_total[start : start + part.size].reshape(part.shape))
        start += part.size
    (
        decay_grad,
        bias_grad,
        skip_grad,
        conv_x_w_grad,
        conv_x_b_grad,
        conv_bc_w_grad,
        conv_bc_b_grad,
    ) = small_sums
    return (
        layer_out,
        tokens_grad,
        gain_one_grad,
        gain_two_grad,
        qkv_grad,
        zx_grad,
        bcd_grad,
        mix_grad,
        gu_grad,
        down_grad,
        decay_grad,
        bias_grad,
        skip_grad,
        conv_x_w_grad,
        conv_x_b_grad,
        conv_bc_w_grad,
        conv_bc_b_grad,
    )


def solution(mesh):
    in_specs = (
        P("dp", "ctx", None),
        P("dp", "ctx"),
        P("dp", "ctx", None),
        P(("dp", "ctx")),
        P(("dp", "ctx")),
        P(("dp", "ctx"), "tp"),
        P(("dp", "ctx"), "tp"),
        P(("dp", "ctx"), None),
        P(("dp", "ctx"), "tp"),
        P(("dp", "ctx"), "tp"),
        P(("dp", "ctx"), "tp"),
        P("tp"),
        P("tp"),
        P("tp"),
        P(None, "tp"),
        P("tp"),
        P(),
        P(),
    )
    out_specs = (
        P("dp", "ctx", None),
        P("dp", "ctx", None),
        P(("dp", "ctx")),
        P(("dp", "ctx")),
        P(("dp", "ctx"), "tp"),
        P(("dp", "ctx"), "tp"),
        P(("dp", "ctx"), None),
        P(("dp", "ctx"), "tp"),
        P(("dp", "ctx"), "tp"),
        P(("dp", "ctx"), "tp"),
        P("tp"),
        P("tp"),
        P("tp"),
        P(None, "tp"),
        P("tp"),
        P(),
        P(),
    )
    return jax.shard_map(
        per_device, mesh=mesh, in_specs=in_specs, out_specs=out_specs, check_vma=False
    )
```

```python
import jax
import jax.numpy as jnp
from jax import lax
from jax.sharding import PartitionSpec as P

HEADS = 8
HEAD_SIZE = 64
M_HEADS = 24
M_HEAD = 64
STATE = 128
FF = 2048


epsilon = 1e-05
rope_base = 100000000000.0
big_negative = -1e30


def carried_in(array, axis, combine, identity):
    count, mine = (lax.axis_size(axis), lax.axis_index(axis))
    everything = jax.tree.map(
        lambda part, kind: lax.all_gather(part.astype(kind), axis),
        array,
        (jnp.bfloat16, jnp.bfloat16, jnp.bfloat16, jnp.bfloat16),
    )
    start = jax.tree.map(
        lambda part, zero: jnp.broadcast_to(jnp.asarray(zero, part.dtype), part.shape),
        array,
        identity,
    )

    def step(k, before):
        reached = k < mine
        new = combine(
            before, jax.tree.map(lambda part, own: part[k].astype(own.dtype), everything, array)
        )
        return jax.tree.map(lambda a, b: jnp.where(reached, a, b), new, before)

    return lax.fori_loop(0, count, step, start)


def prefix(array, axis, join, neutral):
    count = lax.axis_size(axis)
    place = lax.axis_index(axis)
    ahead = count - 1 - place
    gathered = jax.tree.map(
        lambda a, kind: lax.all_gather(a.astype(kind), axis), array, (jnp.bfloat16, jnp.bfloat16)
    )
    state = jax.tree.map(lambda a, e: jnp.zeros_like(a) + jnp.asarray(e, a.dtype), array, neutral)

    def one(step, state):
        source = count - 1 - step
        return join(
            state,
            jax.tree.map(
                lambda a, own: lax.dynamic_index_in_dim(a, source, 0, False).astype(own.dtype),
                gathered,
                array,
            ),
        )

    return lax.fori_loop(0, ahead, one, state)


def shifted(value, axis, steps):
    count = lax.axis_size(axis)
    initial, last = (max(0, -steps), min(count, count - steps))
    return lax.ppermute(value, axis, [(source, source + steps) for source in range(initial, last)])


def pair_sum(partial):
    low = partial.astype(jnp.bfloat16)
    if lax.axis_size("tp") != 2:
        return lax.psum(low, "tp").astype(jnp.float32)
    other = lax.ppermute(low, "tp", [(0, 1), (1, 0)])
    return low.astype(jnp.float32) + other.astype(jnp.float32)


def gather_rows(*shards):
    return [lax.all_gather(shard, ("dp", "ctx"), axis=0, tiled=True) for shard in shards]


def scatter_rows(*partials):
    return [
        lax.psum_scatter(part, ("dp", "ctx"), scatter_dimension=0, tiled=True).astype(jnp.float32)
        for part in partials
    ]


def rms_scale(values):
    return lax.rsqrt(jnp.mean(values * values, -1, keepdims=True) + epsilon)


def norm_back(grad_out, normed, row_scale, gain_vec):
    grad_normed = grad_out * gain_vec
    return row_scale * (grad_normed - normed * jnp.mean(grad_normed * normed, -1, keepdims=True))


def rotate(values, cosine, sine_part):
    half_dim = values.shape[-1] // 2
    front, back_half = (values[..., :half_dim], values[..., half_dim:])
    return jnp.concatenate(
        [front * cosine - back_half * sine_part, back_half * cosine + front * sine_part], -1
    )


def silu_slope(values):
    sigmoid_vals = jax.nn.sigmoid(values)
    return sigmoid_vals * (1.0 + values * (1.0 - sigmoid_vals))


def conv_forward(extended, own_seg, seg_before_ext, weight, bias, count):
    reach = weight.shape[0] - 1
    total = bias
    for lag in range(reach + 1):
        start = reach - lag
        same = (seg_before_ext[:, start : start + count] == own_seg).astype(jnp.float32)
        total = total + weight[lag] * extended[:, start : start + count] * same[..., None]
    return total


def conv_backward(grad_ext, extended, own_seg, seg_before_ext, seg_after_ext, weight, count):
    reach = weight.shape[0] - 1
    own_grad = grad_ext[:, :count]
    input_grad = jnp.zeros_like(own_grad)
    tap_grads = []
    for lag in range(reach + 1):
        ahead = (seg_after_ext[:, lag : lag + count] == own_seg).astype(jnp.float32)
        input_grad = input_grad + weight[lag] * grad_ext[:, lag : lag + count] * ahead[..., None]
        start = reach - lag
        behind = (seg_before_ext[:, start : start + count] == own_seg).astype(jnp.float32)
        tap_grads.append(
            jnp.sum(own_grad * extended[:, start : start + count] * behind[..., None], (0, 1))
        )
    return (input_grad, jnp.stack(tap_grads), jnp.sum(own_grad, (0, 1)))


def link_states(early_part, late_part):
    early_first, early_last, early_gate, early_state = early_part
    late_first, late_last, late_gate, late_state = late_part
    joined = ((early_last == late_first) | (early_last < -0.5) | (late_first < -0.5)).astype(
        jnp.float32
    )
    first_seg = jnp.where(early_first < -0.5, late_first, early_first)
    last_seg = jnp.where(late_last < -0.5, early_last, late_last)
    passing = late_gate * joined[:, None]
    return (
        first_seg,
        last_seg,
        early_gate * passing,
        late_state + passing[:, :, None, None] * early_state,
    )


def link_grads(early_part, late_part):
    early_gate, early_grad = early_part
    late_gate, late_grad = late_part
    return (early_gate * late_gate, late_grad + late_gate[:, :, None, None] * early_grad)


def per_device(
    tokens,
    segment_ids,
    out_grad,
    attn_gain,
    ffn_gain,
    attention_input_weight,
    state_space_input_weight,
    scan_input_weight,
    mixer_output_weight,
    gate_up_weight,
    down_weight_matrix,
    log_decay,
    step_bias,
    skip_gain,
    conv_x_weight,
    conv_x_bias,
    conv_bc_weight,
    conv_bc_bias,
):
    single_layer = jnp.float32
    narrow_slice = jnp.bfloat16
    tp_count = lax.axis_size("tp")
    ctx_count = lax.axis_size("ctx")
    tp_index = lax.axis_index("tp")
    ctx_index = lax.axis_index("ctx")
    sequences, tok_count, model_width = tokens.shape
    head_count = HEADS // tp_count
    mamba_count = M_HEADS // tp_count
    query_width = head_count * HEAD_SIZE
    mamba_width = mamba_count * M_HEAD
    ffn_width = FF // tp_count
    row_count = tok_count * head_count
    score_scale = HEAD_SIZE ** (-0.5)
    reach = conv_x_weight.shape[0] - 1
    qkv_width = attention_input_weight.shape[1]
    zx_width = state_space_input_weight.shape[1]
    bcd_width = scan_input_weight.shape[1]
    first_pad = -(qkv_width + zx_width + bcd_width + 2) % 128
    first_shard = jnp.concatenate(
        [
            state_space_input_weight,
            attention_input_weight,
            scan_input_weight,
            attn_gain[:, None],
            ffn_gain[:, None],
            jnp.zeros((attn_gain.shape[0], first_pad), narrow_slice),
        ],
        1,
    )
    mix_width = mixer_output_weight.shape[1]
    gu_end = mix_width + gate_up_weight.shape[1]
    later_shard = jnp.concatenate(
        [mixer_output_weight, gate_up_weight, down_weight_matrix], 1
    )
    full_first, full_later = gather_rows(first_shard, later_shard)
    full_mix = full_later[:, :mix_width]
    full_gu = full_later[:, mix_width:gu_end]
    full_down = full_later[:, gu_end:]
    first_width = qkv_width + zx_width + bcd_width
    full_zx = full_first[:, :zx_width]
    full_qkv = full_first[:, zx_width : zx_width + qkv_width]
    full_bcd = full_first[:, zx_width + qkv_width : first_width]
    gain_one = full_first[:, first_width].astype(single_layer)
    gain_two = full_first[:, first_width + 1].astype(single_layer)
    layer_inputs = tokens.astype(single_layer)
    first_scale = rms_scale(layer_inputs)
    first_normed = layer_inputs * first_scale
    first_norm_slice = (first_normed * gain_one).astype(narrow_slice)
    qkv_vals = jnp.einsum(
        "btd,dc->btc", first_norm_slice, full_qkv, preferred_element_type=single_layer
    )
    gate_input_values = jnp.einsum(
        "btd,dc->btc", first_norm_slice, full_zx, preferred_element_type=single_layer
    )
    scan_input_values = jnp.einsum(
        "btd,dc->btc", first_norm_slice, full_bcd, preferred_element_type=single_layer
    )
    half_dim = HEAD_SIZE // 2
    frequency = rope_base ** (-jnp.arange(half_dim, dtype=single_layer) * 2.0 / HEAD_SIZE)
    positions = (ctx_index * tok_count + jnp.arange(tok_count, dtype=jnp.int32)).astype(
        single_layer
    )
    angles = positions[:, None] * frequency[None, :]
    cosine, sine_part = (jnp.cos(angles), jnp.sin(angles))
    query_rot = rotate(
        qkv_vals[..., :query_width].reshape(sequences, tok_count, head_count, HEAD_SIZE),
        cosine[None, :, None],
        sine_part[None, :, None],
    )
    query_slice = query_rot.astype(narrow_slice).reshape(sequences, row_count, HEAD_SIZE)
    key_rot = rotate(
        qkv_vals[..., query_width : query_width + HEAD_SIZE], cosine[None], sine_part[None]
    )
    key_value = jnp.concatenate([key_rot, qkv_vals[..., query_width + HEAD_SIZE :]], -1).astype(
        narrow_slice
    )
    seg_float = segment_ids.astype(single_layer)
    conv_x_in = gate_input_values[..., mamba_width:].astype(narrow_slice)
    conv_bc_in = scan_input_values[..., : 2 * STATE].astype(narrow_slice)
    all_kv, all_seg, tails_x, tails_bc = (
        lax.all_gather(key_value, "ctx", axis=1, tiled=True),
        lax.all_gather(seg_float.astype(narrow_slice), "ctx", axis=1, tiled=True),
        lax.all_gather(conv_x_in[:, tok_count - reach :], "ctx", axis=1, tiled=True),
        lax.all_gather(conv_bc_in[:, tok_count - reach :], "ctx", axis=1, tiled=True),
    )
    full_len = all_kv.shape[1]
    seg_all = all_seg.astype(single_layer)
    has_prev = ctx_index > 0
    has_next = ctx_index < ctx_count - 1
    prev_index = jnp.maximum(ctx_index - 1, 0)
    prev_x = lax.dynamic_slice_in_dim(tails_x, prev_index * reach, reach, 1)
    prev_bc = lax.dynamic_slice_in_dim(tails_bc, prev_index * reach, reach, 1)
    prev_x = jnp.where(has_prev, prev_x, jnp.zeros_like(prev_x))
    prev_bc = jnp.where(has_prev, prev_bc, jnp.zeros_like(prev_bc))
    prev_seg = lax.dynamic_slice_in_dim(
        seg_all, jnp.maximum(ctx_index * tok_count - reach, 0), reach, 1
    )
    prev_seg = jnp.where(has_prev, prev_seg, -jnp.ones_like(prev_seg))
    next_seg = lax.dynamic_slice_in_dim(
        seg_all, jnp.minimum((ctx_index + 1) * tok_count, full_len - reach), reach, 1
    )
    next_seg = jnp.where(has_next, next_seg, -jnp.ones_like(next_seg))
    seg_before_ext = jnp.concatenate([prev_seg, seg_float], 1)
    seg_after_ext = jnp.concatenate([seg_float, next_seg], 1)
    ext_x = jnp.concatenate([prev_x, conv_x_in], 1).astype(single_layer)
    ext_bc = jnp.concatenate([prev_bc, conv_bc_in], 1).astype(single_layer)
    conv_x_pre = conv_forward(
        ext_x, seg_float, seg_before_ext, conv_x_weight, conv_x_bias, tok_count
    )
    conv_bc_pre = conv_forward(
        ext_bc, seg_float, seg_before_ext, conv_bc_weight, conv_bc_bias, tok_count
    )
    block_len = min(512, full_len)
    needed = ((ctx_index + 1) * tok_count + block_len - 1) // block_len
    row_pos = ctx_index * tok_count + jnp.arange(row_count, dtype=jnp.int32) // head_count
    row_seg = jnp.repeat(seg_float, head_count, axis=1)

    def block_scores(block_index):
        key_start = block_index * block_len
        key_block_rows = lax.dynamic_slice_in_dim(all_kv, key_start, block_len, 1)
        key_seg = lax.dynamic_slice_in_dim(all_seg, key_start, block_len, 1).astype(single_layer)
        key_pos = key_start + jnp.arange(block_len, dtype=jnp.int32)
        allowed = (key_pos[None, None, :] <= row_pos[None, :, None]) & (
            key_seg[:, None, :] == row_seg[:, :, None]
        )
        raw_scores = (
            jnp.einsum(
                "nwl,nol->nwo",
                query_slice,
                key_block_rows[..., :HEAD_SIZE],
                preferred_element_type=single_layer,
            )
            * score_scale
        )
        return (jnp.where(allowed, raw_scores, big_negative), allowed, key_block_rows)

    def peak_step(block_index, carry):
        row_peak, row_total = carry
        scores, allowed, key_block_rows = block_scores(block_index)
        new_peak = jnp.maximum(row_peak, jnp.max(scores, -1))
        kept = jnp.where(allowed, jnp.exp(scores - new_peak[..., None]), 0.0)
        return (new_peak, row_total * jnp.exp(row_peak - new_peak) + jnp.sum(kept, -1))

    row_peak, row_total = lax.fori_loop(
        0,
        needed,
        peak_step,
        (
            jnp.full((sequences, row_count), big_negative, single_layer),
            jnp.zeros((sequences, row_count), single_layer),
        ),
    )
    log_total = row_peak + jnp.log(row_total)

    def value_step(block_index, accum):
        scores, allowed, key_block_rows = block_scores(block_index)
        probability_slice = jnp.where(allowed, jnp.exp(scores - log_total[..., None]), 0.0).astype(
            narrow_slice
        )
        return accum + jnp.einsum(
            "znw,zwt->znt",
            probability_slice,
            key_block_rows[..., HEAD_SIZE:],
            preferred_element_type=single_layer,
        )

    attn_vals = lax.fori_loop(
        0, needed, value_step, jnp.zeros((sequences, row_count, HEAD_SIZE), single_layer)
    )
    attn_low = attn_vals.astype(narrow_slice).reshape(sequences, tok_count, query_width)
    z_vals = gate_input_values[..., :mamba_width].reshape(sequences, tok_count, mamba_count, M_HEAD)
    xs_low = (
        jax.nn.silu(conv_x_pre)
        .astype(narrow_slice)
        .reshape(sequences, tok_count, mamba_count, M_HEAD)
    )
    xs_vals = xs_low.astype(single_layer)
    bc_low = jax.nn.silu(conv_bc_pre).astype(narrow_slice)
    b_low = bc_low[..., :STATE]
    c_low = bc_low[..., STATE:]
    step_raw = lax.dynamic_slice_in_dim(
        scan_input_values, 2 * STATE + tp_index * mamba_count, mamba_count, 2
    )
    step_size = jax.nn.softplus(step_raw + step_bias)
    decay_rate = jnp.exp(log_decay)
    log_step = -decay_rate * step_size
    cumulative = jnp.cumsum(log_step, 1)
    cum_heads = jnp.moveaxis(cumulative, 2, 1)
    step_heads = jnp.moveaxis(step_size, 2, 1)
    causal = (
        jnp.arange(tok_count, dtype=jnp.int32)[:, None]
        >= jnp.arange(tok_count, dtype=jnp.int32)[None, :]
    )
    same_doc = (seg_float[:, :, None] == seg_float[:, None, :]) & causal[None]
    allowed_heads = same_doc[:, None]
    gap = cum_heads[:, :, :, None] - cum_heads[:, :, None, :]
    expo = jnp.where(allowed_heads, jnp.exp(jnp.where(allowed_heads, gap, 0.0)), 0.0)
    pair = jnp.einsum("btn,bsn->bts", c_low, b_low, preferred_element_type=single_layer)
    mix_matrix = (expo * pair[:, None] * step_heads[:, :, None, :]).astype(narrow_slice)
    intra_term = jnp.einsum(
        "bhts,bshp->bthp", mix_matrix, xs_low, preferred_element_type=single_layer
    )
    end_decay = (
        jnp.exp(cumulative[:, -1:] - cumulative)
        * (seg_float == seg_float[:, -1:]).astype(single_layer)[:, :, None]
    )
    end_weight = end_decay * step_size
    weighted_low = (xs_vals * end_weight[..., None]).astype(narrow_slice)
    local_state = jnp.einsum(
        "bshp,bsn->bhpn", weighted_low, b_low, preferred_element_type=single_layer
    )
    block_gate = (
        jnp.exp(cumulative[:, -1])
        * (seg_float[:, 0] == seg_float[:, -1]).astype(single_layer)[:, None]
    )
    negative = -jnp.ones((sequences,), single_layer)
    identity = (negative, negative, jnp.ones_like(block_gate), jnp.zeros_like(local_state))
    _, seg_before, _, state_before = carried_in(
        (seg_float[:, 0], seg_float[:, -1], block_gate, local_state), "ctx", link_states, identity
    )
    state_low = state_before.astype(narrow_slice)
    inter_term = jnp.einsum("btn,bhpn->bthp", c_low, state_low, preferred_element_type=single_layer)
    entry_decay = (
        jnp.exp(cumulative) * (seg_float == seg_before[:, None]).astype(single_layer)[:, :, None]
    )
    ssm_vals = intra_term + entry_decay[..., None] * inter_term
    mamba_y = ssm_vals + skip_gain[:, None] * xs_vals
    mamba_out = mamba_y * jax.nn.silu(z_vals)
    mixer_slice = jnp.concatenate(
        [mamba_out.reshape(sequences, tok_count, mamba_width).astype(narrow_slice), attn_low], -1
    )
    mix_part = jnp.einsum("btc,dc->btd", mixer_slice, full_mix, preferred_element_type=single_layer)
    middle_state = layer_inputs + pair_sum(mix_part)
    second_scale = rms_scale(middle_state)
    second_normed = middle_state * second_scale
    second_norm_slice = (second_normed * gain_two).astype(narrow_slice)
    gu_vals = jnp.einsum(
        "btd,dc->btc", second_norm_slice, full_gu, preferred_element_type=single_layer
    )
    gate_values, up_vals = (gu_vals[..., :ffn_width], gu_vals[..., ffn_width:])
    activation_slice = (jax.nn.silu(gate_values) * up_vals).astype(narrow_slice)
    ffn_part = jnp.einsum(
        "btc,dc->btd", activation_slice, full_down, preferred_element_type=single_layer
    )
    layer_out = (middle_state + pair_sum(ffn_part)).astype(narrow_slice)
    cotangent = out_grad.astype(single_layer)
    grad_down_w = jnp.einsum(
        "btd,btc->dc", out_grad, activation_slice, preferred_element_type=single_layer
    )
    grad_act = jnp.einsum("btd,dc->btc", out_grad, full_down, preferred_element_type=single_layer)
    grad_gu_low = jnp.concatenate(
        [grad_act * up_vals * silu_slope(gate_values), grad_act * jax.nn.silu(gate_values)], -1
    ).astype(narrow_slice)
    grad_gu_w = jnp.einsum(
        "btd,btc->dc", second_norm_slice, grad_gu_low, preferred_element_type=single_layer
    )
    second_part = jnp.einsum(
        "btc,dc->btd", grad_gu_low, full_gu, preferred_element_type=single_layer
    )
    grad_second = pair_sum(second_part)
    grad_gain_two = jnp.sum(grad_second * second_normed, (0, 1))
    grad_middle = cotangent + norm_back(grad_second, second_normed, second_scale, gain_two)
    grad_mix_low = grad_middle.astype(narrow_slice)
    grad_mix_w = jnp.einsum(
        "btd,btc->dc", grad_mix_low, mixer_slice, preferred_element_type=single_layer
    )
    grad_cat = jnp.einsum(
        "btd,dc->btc", grad_mix_low, full_mix, preferred_element_type=single_layer
    )
    grad_mamba = grad_cat[..., :mamba_width].reshape(sequences, tok_count, mamba_count, M_HEAD)
    attention_gradient_slice = (
        grad_cat[..., mamba_width:].astype(narrow_slice).reshape(sequences, row_count, HEAD_SIZE)
    )
    delta = jnp.sum(attention_gradient_slice.astype(single_layer) * attn_vals, -1)

    def grad_step(block_index, carry):
        grad_query, grad_kv = carry
        scores, allowed, key_block_rows = block_scores(block_index)
        attention_probabilities = jnp.where(allowed, jnp.exp(scores - log_total[..., None]), 0.0)
        grad_probs = jnp.einsum(
            "nwl,nol->nwo",
            attention_gradient_slice,
            key_block_rows[..., HEAD_SIZE:],
            preferred_element_type=single_layer,
        )
        score_gradient = (
            attention_probabilities * (grad_probs - delta[..., None]) * score_scale
        ).astype(narrow_slice)
        grad_query = grad_query + jnp.einsum(
            "znw,zwt->znt",
            score_gradient,
            key_block_rows[..., :HEAD_SIZE],
            preferred_element_type=single_layer,
        )
        grad_keys = jnp.einsum(
            "pni,pnx->pix", score_gradient, query_slice, preferred_element_type=single_layer
        )
        grad_values = jnp.einsum(
            "pni,pnx->pix",
            attention_probabilities.astype(narrow_slice),
            attention_gradient_slice,
            preferred_element_type=single_layer,
        )
        grad_kv = lax.dynamic_update_slice_in_dim(
            grad_kv, jnp.concatenate([grad_keys, grad_values], -1), block_index * block_len, 1
        )
        return (grad_query, grad_kv)

    grad_query, grad_kv = lax.fori_loop(
        0,
        needed,
        grad_step,
        (
            jnp.zeros((sequences, row_count, HEAD_SIZE), single_layer),
            jnp.zeros((sequences, full_len, 2 * HEAD_SIZE), single_layer),
        ),
    )
    own_kv = lax.psum_scatter(
        grad_kv.astype(jnp.bfloat16), "ctx", scatter_dimension=1, tiled=True
    ).astype(jnp.float32)
    query_back = rotate(
        grad_query.reshape(sequences, tok_count, head_count, HEAD_SIZE),
        cosine[None, :, None],
        -sine_part[None, :, None],
    )
    key_back = rotate(own_kv[..., :HEAD_SIZE], cosine[None], -sine_part[None])
    grad_qkv_low = jnp.concatenate(
        [query_back.reshape(sequences, tok_count, query_width), key_back, own_kv[..., HEAD_SIZE:]],
        -1,
    ).astype(narrow_slice)
    sigmoid_z = jax.nn.sigmoid(z_vals)
    grad_y = grad_mamba * z_vals * sigmoid_z
    grad_z = grad_mamba * mamba_y * silu_slope(z_vals)
    grad_skip = jnp.sum(grad_y * xs_vals, (0, 1, 3))
    grad_xs = grad_y * skip_gain[:, None]
    grad_ssm_low = grad_y.astype(narrow_slice)
    grad_matrix = jnp.einsum(
        "bthp,bshp->bhts", grad_ssm_low, xs_low, preferred_element_type=single_layer
    )
    grad_xs = grad_xs + jnp.einsum(
        "bhts,bthp->bshp", mix_matrix, grad_ssm_low, preferred_element_type=single_layer
    )
    shared = grad_matrix * expo
    grad_pair = jnp.sum(shared * step_heads[:, :, None, :], 1)
    grad_step_heads = jnp.sum(shared * pair[:, None], 2)
    grad_gap = shared * pair[:, None] * step_heads[:, :, None, :]
    grad_cum_heads = jnp.sum(grad_gap, 3) - jnp.sum(grad_gap, 2)
    inter_low = (grad_ssm_low.astype(single_layer) * entry_decay[..., None]).astype(narrow_slice)
    grad_entry = jnp.sum(grad_ssm_low.astype(single_layer) * inter_term, -1)
    grad_c = jnp.einsum("bthp,bhpn->btn", inter_low, state_low, preferred_element_type=single_layer)
    grad_state_in = jnp.einsum(
        "bthp,btn->bhpn", inter_low, c_low, preferred_element_type=single_layer
    )
    carry_gate = (seg_float[:, -1] == seg_before).astype(single_layer)[:, None] * jnp.exp(
        cumulative[:, -1]
    )
    _, later_grad = prefix(
        (carry_gate, grad_state_in),
        "ctx",
        link_grads,
        (jnp.ones_like(carry_gate), jnp.zeros_like(grad_state_in)),
    )
    later_low = later_grad.astype(narrow_slice)
    grad_weighted = jnp.einsum(
        "bhpn,bsn->bshp", later_low, b_low, preferred_element_type=single_layer
    )
    grad_b = jnp.einsum(
        "bshp,bhpn->bsn", weighted_low, later_low, preferred_element_type=single_layer
    )
    grad_xs = grad_xs + grad_weighted * end_weight[..., None]
    grad_end = jnp.sum(grad_weighted * xs_vals, -1)
    grad_log_end = grad_end * end_weight
    grad_cum = jnp.moveaxis(grad_cum_heads, 1, 2) + grad_entry * entry_decay - grad_log_end
    grad_cum = grad_cum.at[:, -1].add(
        carry_gate * jnp.sum(later_grad * state_before, (2, 3)) + jnp.sum(grad_log_end, 1)
    )
    pair_low = grad_pair.astype(narrow_slice)
    grad_c = grad_c + jnp.einsum(
        "bts,bsn->btn", pair_low, b_low, preferred_element_type=single_layer
    )
    grad_b = grad_b + jnp.einsum(
        "bts,btn->bsn", pair_low, c_low, preferred_element_type=single_layer
    )
    grad_log_step = jnp.flip(jnp.cumsum(jnp.flip(grad_cum, 1), 1), 1)
    grad_step = (
        jnp.moveaxis(grad_step_heads, 1, 2) + grad_end * end_decay - grad_log_step * decay_rate
    )
    grad_log_decay = jnp.sum(grad_log_step * log_step, (0, 1))
    grad_raw = grad_step * jax.nn.sigmoid(step_raw + step_bias)
    grad_step_bias = jnp.sum(grad_raw, (0, 1))
    grad_steps = lax.dynamic_update_slice_in_dim(
        jnp.zeros((sequences, tok_count, M_HEADS), single_layer),
        grad_raw,
        tp_index * mamba_count,
        2,
    )
    post_x = grad_xs.reshape(sequences, tok_count, mamba_width) * silu_slope(conv_x_pre)
    post_bc = jnp.concatenate([grad_b, grad_c], -1) * silu_slope(conv_bc_pre)
    next_x, next_bc = shifted((post_x[:, :reach], post_bc[:, :reach]), "ctx", -1)
    grad_in_x, conv_x_w_part, conv_x_b_part = conv_backward(
        jnp.concatenate([post_x, next_x], 1),
        ext_x,
        seg_float,
        seg_before_ext,
        seg_after_ext,
        conv_x_weight,
        tok_count,
    )
    grad_zx_low = jnp.concatenate(
        [grad_z.reshape(sequences, tok_count, mamba_width), grad_in_x], -1
    ).astype(narrow_slice)
    first_part = jnp.einsum(
        "btc,dc->btd", grad_qkv_low, full_qkv, preferred_element_type=single_layer
    )
    first_part = first_part + jnp.einsum(
        "btc,dc->btd", grad_zx_low, full_zx, preferred_element_type=single_layer
    )
    first_sum, bc_total, steps_total = (
        pair_sum(first_part),
        pair_sum(jnp.concatenate([post_bc, next_bc], 1)),
        pair_sum(grad_steps),
    )
    grad_in_bc, conv_bc_w_part, conv_bc_b_part = conv_backward(
        bc_total, ext_bc, seg_float, seg_before_ext, seg_after_ext, conv_bc_weight, tok_count
    )
    bcd_low = jnp.concatenate([grad_in_bc, steps_total], -1).astype(narrow_slice)
    grad_first = first_sum + jnp.einsum(
        "btc,dc->btd", bcd_low, full_bcd, preferred_element_type=single_layer
    )
    grad_qkv_w = jnp.einsum(
        "btd,btc->dc", first_norm_slice, grad_qkv_low, preferred_element_type=single_layer
    )
    grad_zx_w = jnp.einsum(
        "btd,btc->dc", first_norm_slice, grad_zx_low, preferred_element_type=single_layer
    )
    grad_bcd_w = jnp.einsum(
        "btd,btc->dc", first_norm_slice, bcd_low, preferred_element_type=single_layer
    )
    grad_gain_one = jnp.sum(grad_first * first_normed, (0, 1))
    tokens_grad = grad_middle + norm_back(grad_first, first_normed, first_scale, gain_one)
    grad_first_w = jnp.concatenate(
        [
            grad_zx_w.astype(narrow_slice),
            grad_qkv_w.astype(narrow_slice),
            grad_bcd_w.astype(narrow_slice),
            grad_gain_one.astype(narrow_slice)[:, None],
            grad_gain_two.astype(narrow_slice)[:, None],
            jnp.zeros((model_width, first_pad), narrow_slice),
        ],
        1,
    )
    grad_later_w = jnp.concatenate(
        [
            grad_mix_w.astype(narrow_slice),
            grad_gu_w.astype(narrow_slice),
            grad_down_w.astype(narrow_slice),
        ],
        1,
    )
    first_own, later_own = scatter_rows(grad_first_w, grad_later_w)
    mix_grad = later_own[:, :mix_width]
    gu_grad = later_own[:, mix_width:gu_end]
    down_grad = later_own[:, gu_end:]
    zx_grad = first_own[:, :zx_width]
    qkv_grad = first_own[:, zx_width : zx_width + qkv_width]
    bcd_grad = first_own[:, zx_width + qkv_width : first_width]
    gain_one_grad = first_own[:, first_width]
    gain_two_grad = first_own[:, first_width + 1]
    small_parts = (
        grad_log_decay,
        grad_step_bias,
        grad_skip,
        conv_x_w_part,
        conv_x_b_part,
        conv_bc_w_part,
        conv_bc_b_part,
    )
    flat = jnp.concatenate([part.reshape(-1) for part in small_parts])
    small_count = flat.shape[0]
    flat = jnp.pad(flat, (0, -small_count % 1024)).reshape(-1, 128)
    small_total = lax.psum(flat, ("dp", "ctx")).reshape(-1)
    small_sums = []
    start = 0
    for part in small_parts:
        small_sums.append(small_total[start : start + part.size].reshape(part.shape))
        start += part.size
    (
        decay_grad,
        bias_grad,
        skip_grad,
        conv_x_w_grad,
        conv_x_b_grad,
        conv_bc_w_grad,
        conv_bc_b_grad,
    ) = small_sums
    return (
        layer_out,
        tokens_grad,
        gain_one_grad,
        gain_two_grad,
        qkv_grad,
        zx_grad,
        bcd_grad,
        mix_grad,
        gu_grad,
        down_grad,
        decay_grad,
        bias_grad,
        skip_grad,
        conv_x_w_grad,
        conv_x_b_grad,
        conv_bc_w_grad,
        conv_bc_b_grad,
    )


def solution(mesh):
    in_specs = (
        P("dp", "ctx", None),
        P("dp", "ctx"),
        P("dp", "ctx", None),
        P(("dp", "ctx")),
        P(("dp", "ctx")),
        P(("dp", "ctx"), "tp"),
        P(("dp", "ctx"), "tp"),
        P(("dp", "ctx"), None),
        P(("dp", "ctx"), "tp"),
        P(("dp", "ctx"), "tp"),
        P(("dp", "ctx"), "tp"),
        P("tp"),
        P("tp"),
        P("tp"),
        P(None, "tp"),
        P("tp"),
        P(),
        P(),
    )
    out_specs = (
        P("dp", "ctx", None),
        P("dp", "ctx", None),
        P(("dp", "ctx")),
        P(("dp", "ctx")),
        P(("dp", "ctx"), "tp"),
        P(("dp", "ctx"), "tp"),
        P(("dp", "ctx"), None),
        P(("dp", "ctx"), "tp"),
        P(("dp", "ctx"), "tp"),
        P(("dp", "ctx"), "tp"),
        P("tp"),
        P("tp"),
        P("tp"),
        P(None, "tp"),
        P("tp"),
        P(),
        P(),
    )
    return jax.shard_map(
        per_device, mesh=mesh, in_specs=in_specs, out_specs=out_specs, check_vma=False
    )
```
